32 devices in a mesh: section: 2 (over y), tp: 16 (over z, x, core).
Axes of the slice: x: 2, y: 2, z: 4, core: 2. Of those that a mesh axis runs over, the one named last changes fastest.
Arguments:
- hidden_in: bfloat16 [2, 512, 4096], P('section', 'tp'), may hold values from -6 to 6
- attn_gain: float32 [2, 4096], P('section'), may hold values from 0.1 to 1.9
- w_query: bfloat16 [2, 4096, 4096], P('section', None, 'tp'), may hold values from -0.21875 to 0.21875
- w_keyval: bfloat16 [2, 4096, 2048], P('section', None, 'tp'), may hold values from -0.09375 to 0.09375
- w_out: bfloat16 [2, 4096, 4096], P('section', 'tp'), may hold values from -0.75 to 0.75
- cache: bfloat16 [2, 8, 65536, 256], P('section', None, 'tp'), may hold values from -96 to 96
- starts: int32 [2], P('section'), may hold values from 16384 to 65536, as said below
- owners: int32 [2, 8, 2, 4], replicated, may hold values from 0 to 31, as said below
Outputs:
- hidden_out: bfloat16 [2, 512, 4096], P('section', 'tp')
- page_pool: bfloat16 [384, 128, 128], P(('section', 'tp'))
The draws below stay inside these ranges and needn't reach their ends.
Inputs may be any that keep to these rules, and one draw needn't show every extreme that they name: `starts`: multiples of 128; one of the two equals 65536. `owners`: every device is named at most 12 times in all, and one device exactly 12 times.
All inputs are finite; a program needn't handle non-finite values.
Results may differ from the reference program's by a relative error of at most 0.02.
The reference program's roundings to bfloat16 on the way (of `normed`, `weights` and `attended`) count: a program that leaves them out, or rounds other values in their place, can miss the bound.
Values may be sent and summed in bfloat16 or wider, within the bound.
A program may use at most 192 MiB of HBM per device.

```python
import math
import jax
import jax.numpy as jnp
from jax import lax

D = 4096
H = 32
KVH = 8
HD = 128
PAGE = 128
DBLOCK = 4
FRESH = 512
PREFIX = 65536
TOTAL = 128
CAP = 12
N_SECTION = 2
DEVICES = 32


def draw_cache(key, part):
    key = jax.random.fold_in(key, 7)
    key_base = jax.random.fold_in(key, 0)
    shape = (N_SECTION, KVH, PREFIX, 2 * HD)
    values = jnp.clip(jax.random.normal(key_base, shape, jnp.float32), -4.0, 4.0)
    return values.astype(jnp.bfloat16)


def draw_starts(key, part):
    key = jax.random.fold_in(key, 3)
    key_vals, key_full = jax.random.split(key)
    picked = jax.random.randint(key_vals, (N_SECTION,), PREFIX // (4 * PAGE), PREFIX // PAGE + 1) * PAGE
    full_one = jax.random.randint(key_full, (), 0, N_SECTION)
    return jnp.where(jnp.arange(N_SECTION) == full_one, PREFIX, picked).astype(jnp.int32)


def draw_owners(key, part):
    key = jax.random.fold_in(key, 5)
    key_hot, key_slots, key_order = jax.random.split(key, 3)
    hottest = jax.random.randint(key_hot, (), 0, DEVICES)
    slots = jax.random.permutation(key_slots, (DEVICES - 1) * CAP)[:TOTAL - CAP]
    others = slots // CAP
    others = others + (others >= hottest).astype(others.dtype)
    listed = jnp.concatenate([jnp.full((CAP,), hottest, others.dtype), others])
    listed = jax.random.permutation(key_order, listed)
    return listed.reshape(N_SECTION, KVH, 2, FRESH // PAGE).astype(jnp.int32)


def level_of(stream_key, shape, shards, low, top_value):
    gain = 1.0
    for axis_at, parts in shards:
        heights = jax.random.uniform(jax.random.fold_in(jax.random.fold_in(stream_key, 6), axis_at), (parts,), jnp.float32, low / len(shards), top_value / len(shards))
        gain = gain * jnp.repeat(jnp.exp(heights), shape[axis_at] // parts).reshape((-1,) + (1,) * (len(shape) - 1 - axis_at))
    return gain


def normal_values(own_key, dims, deviation, reach, cuts=(), kind=jnp.bfloat16):
    loudness = level_of(own_key, dims, cuts, -0.22, 0.18) if cuts else 1.0
    entries = jax.random.normal(own_key, dims, jnp.float32) * deviation * loudness
    return jnp.minimum(jnp.maximum(entries, -reach), reach).astype(kind)


def setup_inputs(seed: int = 0) -> dict:
    streams_of = jax.random.split(jax.random.key(seed), 9)
    return {
        "hidden_in": normal_values(streams_of[0], (N_SECTION, FRESH, D), 1.0, 6.0, ((0, 2), (1, 16))),
        "attn_gain": jnp.clip(1.0 + 0.18 * jax.random.normal(streams_of[1], (N_SECTION, D), jnp.float32), 0.1, 1.9),
        "w_query": normal_values(streams_of[2], (N_SECTION, D, D), (D // 6) ** -0.5, 0.21875, ((0, 2), (2, 16))),
        "w_keyval": normal_values(streams_of[3], (N_SECTION, D, 2 * KVH * HD), D ** -0.5, 0.09375, ((0, 2), (2, 16))),
        "w_out": normal_values(streams_of[4], (N_SECTION, D, D), 64 ** -0.5, 0.75, ((0, 2), (1, 16))),
        "cache": draw_cache(jax.random.fold_in(streams_of[8], 71), 0),
        "starts": draw_starts(jax.random.fold_in(streams_of[8], 71), 0),
        "owners": draw_owners(jax.random.fold_in(streams_of[8], 71), 0),
    }


def rms_norm(values, gain_vec):
    return values * lax.rsqrt(lax.optimization_barrier(jnp.mean(values * values, axis=-1, keepdims=True)) + 1e-06) * gain_vec

def rotate(vectors, positions):
    half_dim = vectors.shape[-1] // 2
    freq_index = jnp.arange(half_dim).astype(jnp.float32)
    inv_freq = jnp.exp(freq_index * (-2.0 * math.log(1000000.0) / vectors.shape[-1]))
    angles = positions.astype(jnp.float32)[:, None] * inv_freq[None, :]
    cosine = jnp.cos(angles)[:, None, :]
    sine = jnp.sin(angles)[:, None, :]
    first_half = vectors[..., :half_dim]
    second_half = vectors[..., half_dim:]
    return jnp.concatenate([first_half * cosine - second_half * sine, second_half * cosine + first_half * sine], axis=-1)

def reference(hidden_in, attn_gain, w_query, w_keyval, w_out, cache, starts, owners):
    group_size = H // KVH
    inv_scale = 1.0 / math.sqrt(HD)
    layer_outs = []
    page_sets = []
    for section_index in range(N_SECTION):
        residual = hidden_in[section_index].astype(jnp.float32)
        normed = rms_norm(residual, attn_gain[section_index]).astype(jnp.bfloat16)
        queries = jnp.dot(normed, w_query[section_index], preferred_element_type=jnp.float32).astype(jnp.bfloat16)
        keyval = jnp.dot(normed, w_keyval[section_index], preferred_element_type=jnp.float32).astype(jnp.bfloat16)
        positions = starts[section_index] + jnp.arange(FRESH, dtype=jnp.int32)
        q_rot = rotate(queries.reshape(FRESH, H, HD).astype(jnp.float32), positions).astype(jnp.bfloat16)
        split_kv = keyval.reshape(FRESH, KVH, 2, HD)
        k_new = rotate(split_kv[:, :, 0].astype(jnp.float32), positions).astype(jnp.bfloat16)
        v_new = split_kv[:, :, 1]
        cached_ok = jnp.arange(PREFIX, dtype=jnp.int32) < starts[section_index]
        row_block = jnp.arange(FRESH, dtype=jnp.int32) // DBLOCK
        fresh_ok = row_block[None, :] <= row_block[:, None]
        visible = jnp.concatenate([jnp.broadcast_to(cached_ok[None, :], (FRESH, PREFIX)), fresh_ok], axis=1)
        section_cache = cache[section_index]

        def head_out(head_index):
            kv_index = head_index // group_size
            cached = lax.dynamic_index_in_dim(section_cache, kv_index, 0, False)
            all_keys = jnp.concatenate([cached[:, :HD], lax.dynamic_index_in_dim(k_new, kv_index, 1, False)], axis=0)
            all_vals = jnp.concatenate([cached[:, HD:], lax.dynamic_index_in_dim(v_new, kv_index, 1, False)], axis=0)
            query_head = lax.dynamic_index_in_dim(q_rot, head_index, 1, False)
            scores = jnp.dot(query_head, all_keys.T, preferred_element_type=jnp.float32) * inv_scale
            scores = jnp.where(visible, scores, -jnp.inf)
            row_top = lax.optimization_barrier(jnp.max(scores, axis=1, keepdims=True))
            expo = jnp.exp(scores - row_top)
            denominator = lax.optimization_barrier(jnp.sum(expo, axis=1, keepdims=True))
            weights = expo.astype(jnp.bfloat16)
            summed = jnp.dot(weights, all_vals, preferred_element_type=jnp.float32)
            return (summed / denominator).astype(jnp.bfloat16)
        heads = lax.map(head_out, jnp.arange(H, dtype=jnp.int32))
        attended = jnp.transpose(heads, (1, 0, 2)).reshape(FRESH, D)
        layer_out = residual + jnp.dot(attended, w_out[section_index], preferred_element_type=jnp.float32)
        layer_outs.append(layer_out.astype(jnp.bfloat16))
        stacked = jnp.stack([k_new, v_new], axis=2)
        stacked = stacked.reshape(FRESH // PAGE, PAGE, KVH, 2, HD)
        page_sets.append(jnp.transpose(stacked, (2, 3, 0, 1, 4)).reshape(-1, PAGE, HD))
    hidden_out = jnp.stack([layer_outs[(section_index - 1) % N_SECTION] for section_index in range(N_SECTION)])
    all_pages = jnp.concatenate(page_sets, axis=0)
    owner_flat = owners.reshape(-1)
    order = jnp.arange(owner_flat.shape[0], dtype=jnp.int32)
    same_owner = owner_flat[:, None] == owner_flat[None, :]
    earlier = order[None, :] < order[:, None]
    slot_rank = lax.optimization_barrier(jnp.sum((same_owner & earlier).astype(jnp.int32), axis=1)).astype(jnp.int32)
    destination = owner_flat * CAP + slot_rank
    page_pool = jnp.zeros((DEVICES * CAP, PAGE, HD), jnp.bfloat16).at[destination].set(all_pages)
    return (hidden_out, page_pool)
```

```python
import math

import jax
import jax.numpy as jnp
from jax import lax
from jax.experimental import pallas as pl
from jax.experimental.pallas import tpu as pltpu
from jax.sharding import PartitionSpec as P

D = 4096
H = 32
KVH = 8
HD = 128
PAGE = 128
DBLOCK = 4
FRESH = 512


def passed_along(block, axis, distance):
    devices = range(lax.axis_size(axis))
    route = [((i - distance) % len(devices), i) for i in devices]
    return lax.ppermute(block, axis, route)


def rms_norm(values, gain_vec):
    return values * lax.rsqrt(jnp.mean(values * values, axis=-1, keepdims=True) + 1e-06) * gain_vec


def rotate(vectors, positions):
    half_dim = vectors.shape[-1] // 2
    freq_index = jnp.arange(half_dim).astype(jnp.float32)
    inv_freq = jnp.exp(freq_index * (-2.0 * math.log(1000000.0) / vectors.shape[-1]))
    angles = positions.astype(jnp.float32)[:, None] * inv_freq[None, :]
    cosine = jnp.cos(angles)[:, None, :]
    sine = jnp.sin(angles)[:, None, :]
    first_half = vectors[..., :half_dim]
    second_half = vectors[..., half_dim:]
    return jnp.concatenate(
        [first_half * cosine - second_half * sine, second_half * cosine + first_half * sine],
        axis=-1,
    )


def pick_pages(page_set, owner_flat, section_slot, target, capacity):
    per_section = page_set.shape[0]
    is_mine = (owner_flat == target).astype(jnp.int32)
    slot_rank = jnp.cumsum(is_mine) - 1
    mine_here = lax.dynamic_slice_in_dim(is_mine, section_slot * per_section, per_section)
    rank_here = lax.dynamic_slice_in_dim(slot_rank, section_slot * per_section, per_section)
    wanted = (mine_here[None, :] == 1) & (rank_here[None, :] == jnp.arange(capacity)[:, None])
    return jnp.einsum(
        "cp,pxd->cxd", wanted.astype(jnp.bfloat16), page_set, preferred_element_type=jnp.float32
    )


def general_body(hidden_in, attn_gain, w_query, w_keyval, w_out, cache, starts, owners):
    tp_count = lax.axis_size("tp")
    section_count = lax.axis_size("section")
    tp_rank = lax.axis_index("tp")
    section_rank = lax.axis_index("section")
    group_size = H // KVH
    local_rows = hidden_in.shape[1]
    query_cols = w_query.shape[2]
    inv_scale = 1.0 / math.sqrt(HD)
    residual = hidden_in[0].astype(jnp.float32)
    normed = rms_norm(residual, attn_gain[0]).astype(jnp.bfloat16)
    query_weight = w_query[0]
    keyval_weight = w_keyval[0]
    rows_piece = lax.all_gather(normed, "tp", axis=0, tiled=True)
    projected = jnp.concatenate(
        [
            jnp.dot(rows_piece, query_weight, preferred_element_type=jnp.float32),
            jnp.dot(rows_piece, keyval_weight, preferred_element_type=jnp.float32),
        ],
        axis=1,
    )
    query_part = projected[:, :query_cols].astype(jnp.bfloat16)
    keyval_part = projected[:, query_cols:].astype(jnp.bfloat16)
    queries, keyval = (
        lax.all_gather(query_part, "tp", axis=1, tiled=True),
        lax.all_gather(keyval_part, "tp", axis=1, tiled=True),
    )
    block_start = starts[0]
    positions = block_start + jnp.arange(FRESH, dtype=jnp.int32)
    q_rot = rotate(queries.reshape(FRESH, H, HD).astype(jnp.float32), positions).astype(
        jnp.bfloat16
    )
    q_rot = q_rot.reshape(FRESH, KVH, group_size, HD)
    split_kv = keyval.reshape(FRESH, KVH, 2, HD)
    k_new = rotate(split_kv[:, :, 0].astype(jnp.float32), positions).astype(jnp.bfloat16)
    v_new = split_kv[:, :, 1]
    slot_count = cache.shape[2]
    fresh_count = FRESH // tp_count
    slot_positions = tp_rank * slot_count + jnp.arange(slot_count, dtype=jnp.int32)
    cached_ok = slot_positions < block_start
    fresh_index = tp_rank * fresh_count + jnp.arange(fresh_count, dtype=jnp.int32)
    row_block = jnp.arange(FRESH, dtype=jnp.int32) // DBLOCK
    fresh_ok = fresh_index[None, :] // DBLOCK <= row_block[:, None]
    fresh_keys = lax.dynamic_slice_in_dim(k_new, tp_rank * fresh_count, fresh_count, 0)
    fresh_vals = lax.dynamic_slice_in_dim(v_new, tp_rank * fresh_count, fresh_count, 0)
    local_cache = cache[0]

    def one_group(group_index, carry):
        tops, totals, sums = carry
        query_group = lax.dynamic_index_in_dim(q_rot, group_index, 1, False)
        cached = lax.dynamic_index_in_dim(local_cache, group_index, 0, False)
        cached_keys = cached[:, :HD]
        cached_vals = cached[:, HD:]
        new_keys = lax.dynamic_index_in_dim(fresh_keys, group_index, 1, False)
        new_vals = lax.dynamic_index_in_dim(fresh_vals, group_index, 1, False)
        cached_scores = (
            jnp.einsum("rqd,kd->rqk", query_group, cached_keys, preferred_element_type=jnp.float32)
            * inv_scale
        )
        new_scores = (
            jnp.einsum("rqd,kd->rqk", query_group, new_keys, preferred_element_type=jnp.float32)
            * inv_scale
        )
        cached_scores = jnp.where(cached_ok[None, None, :], cached_scores, -jnp.inf)
        new_scores = jnp.where(fresh_ok[:, None, :], new_scores, -jnp.inf)
        row_top = jnp.maximum(jnp.max(cached_scores, axis=-1), jnp.max(new_scores, axis=-1))
        shift_by = jnp.where(row_top > -jnp.inf, row_top, 0.0)
        cached_weights = jnp.exp(cached_scores - shift_by[..., None])
        new_weights = jnp.exp(new_scores - shift_by[..., None])
        weight_sum = jnp.sum(cached_weights, axis=-1) + jnp.sum(new_weights, axis=-1)
        value_sum = jnp.einsum(
            "rqk,kd->rqd",
            cached_weights.astype(jnp.bfloat16),
            cached_vals,
            preferred_element_type=jnp.float32,
        )
        value_sum = value_sum + jnp.einsum(
            "rqk,kd->rqd",
            new_weights.astype(jnp.bfloat16),
            new_vals,
            preferred_element_type=jnp.float32,
        )
        tops = lax.dynamic_update_index_in_dim(tops, row_top, group_index, 1)
        totals = lax.dynamic_update_index_in_dim(totals, weight_sum, group_index, 1)
        sums = lax.dynamic_update_index_in_dim(sums, value_sum, group_index, 1)
        return (tops, totals, sums)

    initial = (
        jnp.full((FRESH, KVH, group_size), -jnp.inf, jnp.float32),
        jnp.zeros((FRESH, KVH, group_size), jnp.float32),
        jnp.zeros((FRESH, KVH, group_size, HD), jnp.float32),
    )
    tops, totals, sums = lax.fori_loop(0, KVH, one_group, initial)
    tops = tops.reshape(FRESH, H)
    totals = totals.reshape(FRESH, H)
    peak = lax.pmax(tops.astype(jnp.bfloat16), "tp").astype(tops.dtype)
    factor = jnp.where(tops > -jnp.inf, jnp.exp(tops - peak), 0.0)
    scaled = (sums.reshape(FRESH, H, HD) * factor[:, :, None]).reshape(FRESH, D)
    head_share = lax.psum_scatter(scaled, "tp", scatter_dimension=1, tiled=True)
    weight_total = lax.psum(totals * factor, "tp")
    share_cols = head_share.shape[1]
    heads_here = max(share_cols // HD, 1)
    first_head = tp_rank * share_cols // HD
    denominator = lax.dynamic_slice_in_dim(weight_total, first_head, heads_here, 1)
    attended = (
        head_share.reshape(FRESH, heads_here, share_cols // heads_here) / denominator[:, :, None]
    )
    attended = attended.reshape(FRESH, share_cols).astype(jnp.bfloat16)
    out_weight = w_out[0]
    full_sum = lax.psum(jnp.dot(attended, out_weight, preferred_element_type=jnp.float32), "tp")
    projected_rows = lax.dynamic_slice_in_dim(full_sum, tp_rank * local_rows, local_rows, 0)
    layer_out = (residual + projected_rows).astype(jnp.bfloat16)
    passed_on = passed_along(layer_out, "section", 1)
    stacked = jnp.stack([k_new, v_new], axis=2).reshape(FRESH // PAGE, PAGE, KVH, 2, HD)
    local_pages = jnp.transpose(stacked, (2, 3, 0, 1, 4)).reshape(-1, PAGE, HD)
    owner_flat = owners.reshape(-1)
    capacity = 3 * max(owner_flat.shape[0] // (section_count * tp_count), 1)
    self_index = section_rank * tp_count + tp_rank
    page_slots = pick_pages(local_pages, owner_flat, section_rank, self_index, capacity)
    prior_section = (section_rank + section_count - 1) % section_count
    earlier_pages = passed_along(local_pages, "section", 1)
    page_slots = page_slots + pick_pages(
        earlier_pages, owner_flat, prior_section, self_index, capacity
    )
    return (passed_on[None], page_slots.astype(jnp.bfloat16))


NEG = -1e30
CHUNKS = 2
ROW_TILE = 256
TILES = 4


def attend_kernel(count_ref, q_ref, kv_ref, sums_ref, lse_ref, *, tile, scale):
    slots = kv_ref.shape[1]
    rows = q_ref.shape[1]
    count = count_ref[0]

    def run(masked):
        keys = kv_ref[0, :, :HD]
        vals = kv_ref[0, :, HD:]
        vals_one = jnp.concatenate([vals, jnp.ones_like(vals)], axis=1)
        if masked:
            seen = lax.broadcasted_iota(jnp.int32, (1, slots), 1) < count

        def scores_of(at):
            return lax.dot_general(
                q_ref[0, at * tile : (at + 1) * tile, :],
                keys,
                (((1,), (1,)), ((), ())),
                preferred_element_type=jnp.float32,
            )

        scores = scores_of(0)
        for at in range(rows // tile):
            later = scores_of(at + 1) if at + 1 < rows // tile else None
            if masked:
                scores = jnp.where(seen, scores, NEG)
            top = jnp.max(scores, axis=1, keepdims=True)
            weights = jnp.exp2((scores - top) * scale)
            if masked:
                weights = jnp.where(seen, weights, 0.0)
            both = jnp.dot(
                weights.astype(jnp.bfloat16), vals_one, preferred_element_type=jnp.float32
            )
            total = both[:, HD:]
            safe = jnp.where(total > 0.0, total, 1.0)
            sums_ref[0, at * tile : (at + 1) * tile, :] = both[:, :HD] / safe
            lse = jnp.where(total > 0.0, top * scale + jnp.log2(safe), NEG)
            lse_ref[0, 0:1, at * tile : (at + 1) * tile] = jnp.transpose(lse)[0:1, :]
            scores = later

    @pl.when(count == slots)
    def _():
        run(False)

    @pl.when((count > 0) & (count < slots))
    def _():
        run(True)

    @pl.when(count == 0)
    def _():
        sums_ref[...] = jnp.zeros_like(sums_ref)
        lse_ref[...] = jnp.full_like(lse_ref, NEG)


def attend(q_all, local_cache, count):
    groups, rows, _ = q_all.shape
    slots = local_cache.shape[1]
    tile = min(ROW_TILE, rows)
    block = min(tile * TILES, rows)
    scale = math.log2(math.e) / math.sqrt(HD)
    return pl.pallas_call(
        lambda *refs: attend_kernel(*refs, tile=tile, scale=scale),
        grid_spec=pltpu.PrefetchScalarGridSpec(
            num_scalar_prefetch=1,
            grid=(groups, rows // block),
            in_specs=[
                pl.BlockSpec((1, block, HD), lambda g, r, n: (g, r, 0)),
                pl.BlockSpec((1, slots, 2 * HD), lambda g, r, n: (g, 0, 0)),
            ],
            out_specs=[
                pl.BlockSpec((1, block, HD), lambda g, r, n: (g, r, 0)),
                pl.BlockSpec((1, 1, block), lambda g, r, n: (g, 0, r)),
            ],
        ),
        out_shape=[
            jax.ShapeDtypeStruct((groups, rows, HD), jnp.float32),
            jax.ShapeDtypeStruct((groups, 1, rows), jnp.float32),
        ],
        compiler_params=pltpu.CompilerParams(vmem_limit_bytes=50 * 1024 * 1024),
        cost_estimate=pl.CostEstimate(
            flops=4 * groups * rows * slots * HD,
            bytes_accessed=groups * slots * HD * 4 + groups * rows * HD * 6,
            transcendentals=groups * rows * slots,
        ),
    )(count, q_all, local_cache)


def take_pages(pages, owner_flat, target, capacity):
    mine = owner_flat == target
    rank = jnp.cumsum(mine.astype(jnp.int32)) - 1
    wanted = mine[None, :] & (rank[None, :] == jnp.arange(capacity)[:, None])
    picked = jnp.sum(jnp.where(wanted, jnp.arange(mine.shape[0])[None, :], 0), axis=1)
    filled = jnp.any(wanted, axis=1)
    taken = [lax.dynamic_index_in_dim(pages, picked[k], 0, True) for k in range(capacity)]
    return jnp.where(filled[:, None, None], jnp.concatenate(taken, axis=0), 0)


def body(hidden_in, attn_gain, w_query, w_keyval, w_out, cache, starts, owners):
    query_cols = w_query.shape[2]
    keyval_cols = w_keyval.shape[2]
    if query_cols != 2 * HD or keyval_cols != HD:
        return general_body(
            hidden_in, attn_gain, w_query, w_keyval, w_out, cache, starts, owners
        )
    tp_count = lax.axis_size("tp")
    section_count = lax.axis_size("section")
    tp_rank = lax.axis_index("tp")
    section_rank = lax.axis_index("section")
    local_rows = hidden_in.shape[1]
    heads_here = query_cols // HD
    scale = math.log2(math.e) / math.sqrt(HD)
    residual = hidden_in[0].astype(jnp.float32)
    normed = rms_norm(residual, attn_gain[0]).astype(jnp.bfloat16)
    all_rows = lax.all_gather(normed, "tp", axis=0, tiled=True)
    block_start = starts[0]
    positions = block_start + jnp.arange(FRESH, dtype=jnp.int32)
    queries = jnp.dot(all_rows, w_query[0], preferred_element_type=jnp.float32)
    queries = queries.astype(jnp.bfloat16).astype(jnp.float32)
    q_rot = rotate(queries.reshape(FRESH, heads_here, HD), positions).astype(jnp.bfloat16)
    q_rot = jnp.transpose(q_rot, (1, 0, 2))
    keyval = jnp.dot(all_rows, w_keyval[0], preferred_element_type=jnp.float32)
    keyval = keyval.astype(jnp.bfloat16)
    turned = rotate(keyval.astype(jnp.float32)[:, None, :], positions)[:, 0]
    holds_key = tp_rank % 2 == 0
    part = jnp.where(holds_key, turned.astype(jnp.bfloat16), keyval)
    pair = [(i, i ^ 1) for i in range(tp_count)]
    other = lax.ppermute(part, "tp", pair)
    fresh_key = jnp.where(holds_key, part, other)
    fresh_val = jnp.where(holds_key, other, part)

    step = local_rows // CHUNKS
    by_chunk = q_rot.reshape(heads_here, tp_count, CHUNKS, step, HD)
    part_rows = tp_count * step
    slots = cache.shape[2]
    count = jnp.clip(block_start - tp_rank * slots, 0, slots).reshape(1)
    local_cache = cache[0]
    token = jnp.arange(FRESH, dtype=jnp.int32).reshape(tp_count, CHUNKS, step)
    gathered = [
        lax.all_gather(
            by_chunk[:, :, c].reshape(heads_here, part_rows, HD), "tp", axis=0, tiled=True
        )
        for c in range(CHUNKS)
    ]
    outs = []
    for c in range(CHUNKS):
        q_all = gathered[c].reshape(KVH, H // KVH * part_rows, HD)
        sums, lse = attend(q_all, local_cache, count)
        sums = sums.reshape(H, part_rows, HD)
        lse = lse.reshape(H, part_rows)
        lses = lax.all_gather(lse, "tp", axis=0)
        peak = jnp.max(lses, axis=0)
        whole = peak + jnp.log2(jnp.sum(jnp.exp2(lses - peak[None]), axis=0))
        scaled = sums * jnp.exp2(lse - whole)[:, :, None]
        share = lax.psum_scatter(scaled, "tp", scatter_dimension=0, tiled=True)
        whole_here = lax.dynamic_slice_in_dim(whole, tp_rank * heads_here, heads_here, 0)
        mine = by_chunk[:, :, c].reshape(heads_here, part_rows, HD)
        new_scores = jnp.einsum(
            "hrd,kd->hrk", mine, fresh_key, preferred_element_type=jnp.float32
        )
        row_block = token[:, c].reshape(part_rows) // DBLOCK
        fresh_ok = jnp.arange(FRESH, dtype=jnp.int32)[None, :] // DBLOCK <= row_block[:, None]
        new_scores = jnp.where(fresh_ok[None], new_scores * scale, NEG)
        new_top = jnp.max(new_scores, axis=-1, keepdims=True)
        new_weights = jnp.exp2(new_scores - new_top)
        new_total = jnp.sum(new_weights, axis=-1)
        new_sums = jnp.einsum(
            "hrk,kd->hrd",
            new_weights.astype(jnp.bfloat16),
            fresh_val,
            preferred_element_type=jnp.float32,
        )
        joint = jnp.maximum(new_top[..., 0], whole_here)
        old_part = jnp.exp2(whole_here - joint)
        new_part = jnp.exp2(new_top[..., 0] - joint)
        attended = (share * old_part[..., None] + new_sums * new_part[..., None]) / (
            old_part + new_total * new_part
        )[..., None]
        attended = jnp.transpose(attended.astype(jnp.bfloat16), (1, 0, 2))
        attended = attended.reshape(part_rows, query_cols)
        product = jnp.dot(attended, w_out[0], preferred_element_type=jnp.float32)
        outs.append(lax.psum_scatter(product, "tp", scatter_dimension=0, tiled=True))
    projected_rows = jnp.stack(outs, axis=0).reshape(local_rows, D)
    layer_out = (residual + projected_rows).astype(jnp.bfloat16)
    passed_on = passed_along(layer_out, "section", 1)

    pages = lax.all_gather(part, ("section", "tp"), axis=0, tiled=True)
    pages = pages.reshape(-1, PAGE, HD)
    owner_flat = owners.reshape(-1)
    capacity = 3 * max(owner_flat.shape[0] // (section_count * tp_count), 1)
    self_index = section_rank * tp_count + tp_rank
    return (passed_on[None], take_pages(pages, owner_flat, self_index, capacity))


def solution(mesh):
    in_specs = (
        P("section", "tp", None),
        P("section", None),
        P("section", None, "tp"),
        P("section", None, "tp"),
        P("section", "tp", None),
        P("section", None, "tp", None),
        P("section"),
        P(),
    )
    out_specs = (P("section", "tp", None), P(("section", "tp"), None, None))
    return jax.shard_map(body, mesh=mesh, in_specs=in_specs, out_specs=out_specs, check_vma=False)
```

```python
import math

import jax
import jax.numpy as jnp
from jax import lax
from jax.experimental import pallas as pl
from jax.experimental.pallas import tpu as pltpu
from jax.sharding import PartitionSpec as P

D = 4096
H = 32
KVH = 8
HD = 128
PAGE = 128
DBLOCK = 4
FRESH = 512


def passed_along(block, axis, distance):
    devices = range(lax.axis_size(axis))
    route = [((i - distance) % len(devices), i) for i in devices]
    return lax.ppermute(block, axis, route)


def rms_norm(values, gain_vec):
    return values * lax.rsqrt(jnp.mean(values * values, axis=-1, keepdims=True) + 1e-06) * gain_vec


def rotate(vectors, positions):
    half_dim = vectors.shape[-1] // 2
    freq_index = jnp.arange(half_dim).astype(jnp.float32)
    inv_freq = jnp.exp(freq_index * (-2.0 * math.log(1000000.0) / vectors.shape[-1]))
    angles = positions.astype(jnp.float32)[:, None] * inv_freq[None, :]
    cosine = jnp.cos(angles)[:, None, :]
    sine = jnp.sin(angles)[:, None, :]
    first_half = vectors[..., :half_dim]
    second_half = vectors[..., half_dim:]
    return jnp.concatenate(
        [first_half * cosine - second_half * sine, second_half * cosine + first_half * sine],
        axis=-1,
    )


def pick_pages(page_set, owner_flat, section_slot, target, capacity):
    per_section = page_set.shape[0]
    is_mine = (owner_flat == target).astype(jnp.int32)
    slot_rank = jnp.cumsum(is_mine) - 1
    mine_here = lax.dynamic_slice_in_dim(is_mine, section_slot * per_section, per_section)
    rank_here = lax.dynamic_slice_in_dim(slot_rank, section_slot * per_section, per_section)
    wanted = (mine_here[None, :] == 1) & (rank_here[None, :] == jnp.arange(capacity)[:, None])
    return jnp.einsum(
        "cp,pxd->cxd", wanted.astype(jnp.bfloat16), page_set, preferred_element_type=jnp.float32
    )


def general_body(hidden_in, attn_gain, w_query, w_keyval, w_out, cache, starts, owners):
    tp_count = lax.axis_size("tp")
    section_count = lax.axis_size("section")
    tp_rank = lax.axis_index("tp")
    section_rank = lax.axis_index("section")
    group_size = H // KVH
    local_rows = hidden_in.shape[1]
    query_cols = w_query.shape[2]
    inv_scale = 1.0 / math.sqrt(HD)
    residual = hidden_in[0].astype(jnp.float32)
    normed = rms_norm(residual, attn_gain[0]).astype(jnp.bfloat16)
    query_weight = w_query[0]
    keyval_weight = w_keyval[0]
    rows_piece = lax.all_gather(normed, "tp", axis=0, tiled=True)
    projected = jnp.concatenate(
        [
            jnp.dot(rows_piece, query_weight, preferred_element_type=jnp.float32),
            jnp.dot(rows_piece, keyval_weight, preferred_element_type=jnp.float32),
        ],
        axis=1,
    )
    query_part = projected[:, :query_cols].astype(jnp.bfloat16)
    keyval_part = projected[:, query_cols:].astype(jnp.bfloat16)
    queries, keyval = (
        lax.all_gather(query_part, "tp", axis=1, tiled=True),
        lax.all_gather(keyval_part, "tp", axis=1, tiled=True),
    )
    block_start = starts[0]
    positions = block_start + jnp.arange(FRESH, dtype=jnp.int32)
    q_rot = rotate(queries.reshape(FRESH, H, HD).astype(jnp.float32), positions).astype(
        jnp.bfloat16
    )
    q_rot = q_rot.reshape(FRESH, KVH, group_size, HD)
    split_kv = keyval.reshape(FRESH, KVH, 2, HD)
    k_new = rotate(split_kv[:, :, 0].astype(jnp.float32), positions).astype(jnp.bfloat16)
    v_new = split_kv[:, :, 1]
    slot_count = cache.shape[2]
    fresh_count = FRESH // tp_count
    slot_positions = tp_rank * slot_count + jnp.arange(slot_count, dtype=jnp.int32)
    cached_ok = slot_positions < block_start
    fresh_index = tp_rank * fresh_count + jnp.arange(fresh_count, dtype=jnp.int32)
    row_block = jnp.arange(FRESH, dtype=jnp.int32) // DBLOCK
    fresh_ok = fresh_index[None, :] // DBLOCK <= row_block[:, None]
    fresh_keys = lax.dynamic_slice_in_dim(k_new, tp_rank * fresh_count, fresh_count, 0)
    fresh_vals = lax.dynamic_slice_in_dim(v_new, tp_rank * fresh_count, fresh_count, 0)
    local_cache = cache[0]

    def one_group(group_index, carry):
        tops, totals, sums = carry
        query_group = lax.dynamic_index_in_dim(q_rot, group_index, 1, False)
        cached = lax.dynamic_index_in_dim(local_cache, group_index, 0, False)
        cached_keys = cached[:, :HD]
        cached_vals = cached[:, HD:]
        new_keys = lax.dynamic_index_in_dim(fresh_keys, group_index, 1, False)
        new_vals = lax.dynamic_index_in_dim(fresh_vals, group_index, 1, False)
        cached_scores = (
            jnp.einsum("rqd,kd->rqk", query_group, cached_keys, preferred_element_type=jnp.float32)
            * inv_scale
        )
        new_scores = (
            jnp.einsum("rqd,kd->rqk", query_group, new_keys, preferred_element_type=jnp.float32)
            * inv_scale
        )
        cached_scores = jnp.where(cached_ok[None, None, :], cached_scores, -jnp.inf)
        new_scores = jnp.where(fresh_ok[:, None, :], new_scores, -jnp.inf)
        row_top = jnp.maximum(jnp.max(cached_scores, axis=-1), jnp.max(new_scores, axis=-1))
        shift_by = jnp.where(row_top > -jnp.inf, row_top, 0.0)
        cached_weights = jnp.exp(cached_scores - shift_by[..., None])
        new_weights = jnp.exp(new_scores - shift_by[..., None])
        weight_sum = jnp.sum(cached_weights, axis=-1) + jnp.sum(new_weights, axis=-1)
        value_sum = jnp.einsum(
            "rqk,kd->rqd",
            cached_weights.astype(jnp.bfloat16),
            cached_vals,
            preferred_element_type=jnp.float32,
        )
        value_sum = value_sum + jnp.einsum(
            "rqk,kd->rqd",
            new_weights.astype(jnp.bfloat16),
            new_vals,
            preferred_element_type=jnp.float32,
        )
        tops = lax.dynamic_update_index_in_dim(tops, row_top, group_index, 1)
        totals = lax.dynamic_update_index_in_dim(totals, weight_sum, group_index, 1)
        sums = lax.dynamic_update_index_in_dim(sums, value_sum, group_index, 1)
        return (tops, totals, sums)

    initial = (
        jnp.full((FRESH, KVH, group_size), -jnp.inf, jnp.float32),
        jnp.zeros((FRESH, KVH, group_size), jnp.float32),
        jnp.zeros((FRESH, KVH, group_size, HD), jnp.float32),
    )
    tops, totals, sums = lax.fori_loop(0, KVH, one_group, initial)
    tops = tops.reshape(FRESH, H)
    totals = totals.reshape(FRESH, H)
    peak = lax.pmax(tops.astype(jnp.bfloat16), "tp").astype(tops.dtype)
    factor = jnp.where(tops > -jnp.inf, jnp.exp(tops - peak), 0.0)
    scaled = (sums.reshape(FRESH, H, HD) * factor[:, :, None]).reshape(FRESH, D)
    head_share = lax.psum_scatter(scaled, "tp", scatter_dimension=1, tiled=True)
    weight_total = lax.psum(totals * factor, "tp")
    share_cols = head_share.shape[1]
    heads_here = max(share_cols // HD, 1)
    first_head = tp_rank * share_cols // HD
    denominator = lax.dynamic_slice_in_dim(weight_total, first_head, heads_here, 1)
    attended = (
        head_share.reshape(FRESH, heads_here, share_cols // heads_here) / denominator[:, :, None]
    )
    attended = attended.reshape(FRESH, share_cols).astype(jnp.bfloat16)
    out_weight = w_out[0]
    full_sum = lax.psum(jnp.dot(attended, out_weight, preferred_element_type=jnp.float32), "tp")
    projected_rows = lax.dynamic_slice_in_dim(full_sum, tp_rank * local_rows, local_rows, 0)
    layer_out = (residual + projected_rows).astype(jnp.bfloat16)
    passed_on = passed_along(layer_out, "section", 1)
    stacked = jnp.stack([k_new, v_new], axis=2).reshape(FRESH // PAGE, PAGE, KVH, 2, HD)
    local_pages = jnp.transpose(stacked, (2, 3, 0, 1, 4)).reshape(-1, PAGE, HD)
    owner_flat = owners.reshape(-1)
    capacity = 3 * max(owner_flat.shape[0] // (section_count * tp_count), 1)
    self_index = section_rank * tp_count + tp_rank
    page_slots = pick_pages(local_pages, owner_flat, section_rank, self_index, capacity)
    prior_section = (section_rank + section_count - 1) % section_count
    earlier_pages = passed_along(local_pages, "section", 1)
    page_slots = page_slots + pick_pages(
        earlier_pages, owner_flat, prior_section, self_index, capacity
    )
    return (passed_on[None], page_slots.astype(jnp.bfloat16))


NEG = -1e30
CHUNKS = 1
ROW_TILE = 256
TILES = 4


def attend_kernel(count_ref, q_ref, kv_ref, sums_ref, lse_ref, *, tile, scale):
    slots = kv_ref.shape[1]
    rows = q_ref.shape[1]
    count = count_ref[0]

    def run(masked):
        keys = kv_ref[0, :, :HD]
        vals = kv_ref[0, :, HD:]
        vals_one = jnp.concatenate([vals, jnp.ones_like(vals)], axis=1)
        if masked:
            seen = lax.broadcasted_iota(jnp.int32, (1, slots), 1) < count

        def scores_of(at):
            return lax.dot_general(
                q_ref[0, at * tile : (at + 1) * tile, :],
                keys,
                (((1,), (1,)), ((), ())),
                preferred_element_type=jnp.float32,
            )

        scores = scores_of(0)
        for at in range(rows // tile):
            later = scores_of(at + 1) if at + 1 < rows // tile else None
            if masked:
                scores = jnp.where(seen, scores, NEG)
            top = jnp.max(scores, axis=1, keepdims=True)
            weights = jnp.exp2((scores - top) * scale)
            if masked:
                weights = jnp.where(seen, weights, 0.0)
            both = jnp.dot(
                weights.astype(jnp.bfloat16), vals_one, preferred_element_type=jnp.float32
            )
            total = both[:, HD:]
            safe = jnp.where(total > 0.0, total, 1.0)
            sums_ref[0, at * tile : (at + 1) * tile, :] = both[:, :HD] / safe
            lse = jnp.where(total > 0.0, top * scale + jnp.log2(safe), NEG)
            lse_ref[0, 0:1, at * tile : (at + 1) * tile] = jnp.transpose(lse)[0:1, :]
            scores = later

    @pl.when(count == slots)
    def _():
        run(False)

    @pl.when((count > 0) & (count < slots))
    def _():
        run(True)

    @pl.when(count == 0)
    def _():
        sums_ref[...] = jnp.zeros_like(sums_ref)
        lse_ref[...] = jnp.full_like(lse_ref, NEG)


def attend(q_all, local_cache, count):
    groups, rows, _ = q_all.shape
    slots = local_cache.shape[1]
    tile = min(ROW_TILE, rows)
    block = min(tile * TILES, rows)
    scale = math.log2(math.e) / math.sqrt(HD)
    return pl.pallas_call(
        lambda *refs: attend_kernel(*refs, tile=tile, scale=scale),
        grid_spec=pltpu.PrefetchScalarGridSpec(
            num_scalar_prefetch=1,
            grid=(groups, rows // block),
            in_specs=[
                pl.BlockSpec((1, block, HD), lambda g, r, n: (g, r, 0)),
                pl.BlockSpec((1, slots, 2 * HD), lambda g, r, n: (g, 0, 0)),
            ],
            out_specs=[
                pl.BlockSpec((1, block, HD), lambda g, r, n: (g, r, 0)),
                pl.BlockSpec((1, 1, block), lambda g, r, n: (g, 0, r)),
            ],
        ),
        out_shape=[
            jax.ShapeDtypeStruct((groups, rows, HD), jnp.float32),
            jax.ShapeDtypeStruct((groups, 1, rows), jnp.float32),
        ],
        compiler_params=pltpu.CompilerParams(vmem_limit_bytes=50 * 1024 * 1024),
        cost_estimate=pl.CostEstimate(
            flops=4 * groups * rows * slots * HD,
            bytes_accessed=groups * slots * HD * 4 + groups * rows * HD * 6,
            transcendentals=groups * rows * slots,
        ),
    )(count, q_all, local_cache)


def places(tp_count):
    me = lax.axis_index("tp")
    zs = tp_count // 4
    core, x, z = me % 2, (me // 2) % 2, me // 4

    def at(step, flip_x, flip_core):
        x_at = 1 - x if flip_x else x
        core_at = 1 - core if flip_core else core
        return ((z + step + zs) % zs) * 4 + x_at * 2 + core_at

    return zs, at


def greet(peers):
    barrier = pltpu.get_barrier_semaphore()
    for peer in peers:
        pl.semaphore_signal(
            barrier, inc=1, device_id={"tp": peer}, device_id_type=pl.DeviceIdType.MESH
        )
    pl.semaphore_wait(barrier, len(peers))


def send(src, dst, send_sems, recv_sems, slot, peer):
    return pltpu.make_async_remote_copy(
        src_ref=src,
        dst_ref=dst,
        send_sem=send_sems.at[slot],
        recv_sem=recv_sems.at[slot],
        device_id={"tp": peer},
        device_id_type=pl.DeviceIdType.MESH,
    )


def gather_kernel(own_ref, all_ref, send_sems, recv_sems, own_sem, *, tp_count):
    zs, at = places(tp_count)
    me = at(0, False, False)
    x_peer, core_peer = at(0, True, False), at(0, False, True)
    greet([x_peer, core_peer] + [at(k, False, False) for k in range(1, zs)])
    first_x, first_core = zs - 1, 2 * zs - 1
    started = {}

    def put(src, block, slot, peer):
        started[slot] = send(src, all_ref.at[block], send_sems, recv_sems, slot, peer)
        started[slot].start()

    keep = pltpu.make_async_copy(own_ref, all_ref.at[me], own_sem)
    keep.start()
    put(own_ref, me, first_x, x_peer)
    for k in range(1, zs):
        put(own_ref, me, k - 1, at(k, False, False))
    put(own_ref, me, first_core, core_peer)
    order = [1, zs - 1] + list(range(2, zs - 1))

    def x_arrived(k):
        block = at(-k, True, False)
        started[first_x + k].wait_recv()
        put(all_ref.at[block], block, first_core + zs + k, core_peer)

    for k in order:
        block = at(-k, False, False)
        started[k - 1].wait_recv()
        put(all_ref.at[block], block, first_x + k, x_peer)
        put(all_ref.at[block], block, first_core + k, core_peer)
        if k == order[0]:
            x_arrived(0)
    for k in order:
        x_arrived(k)
    for slot in range(first_core, first_core + 2 * zs):
        started[slot].wait_recv()
    for slot in range(first_core + 2 * zs):
        started[slot].wait_send()
    keep.wait()


def gather_all(own, collective_id):
    tp_count = lax.axis_size("tp")
    copies = tp_count - 1
    return pl.pallas_call(
        lambda *refs: gather_kernel(*refs, tp_count=tp_count),
        out_shape=jax.ShapeDtypeStruct((tp_count,) + own.shape, own.dtype),
        in_specs=[pl.BlockSpec(memory_space=pl.ANY)],
        out_specs=pl.BlockSpec(memory_space=pl.ANY),
        scratch_shapes=[
            pltpu.SemaphoreType.DMA((copies,)),
            pltpu.SemaphoreType.DMA((copies,)),
            pltpu.SemaphoreType.DMA,
        ],
        compiler_params=pltpu.CompilerParams(
            collective_id=collective_id, has_side_effects=True
        ),
    )(own)


def reduce_kernel(
    parts_ref, sum_ref, core_in, x_out, x_in, z_out, z_in, send_sems, recv_sems, *, tp_count
):
    zs, at = places(tp_count)
    x_peer, core_peer = at(0, True, False), at(0, False, True)
    greet([x_peer, core_peer] + [at(k, False, False) for k in range(1, zs)])
    order = list(range(1, zs)) + [0]
    first_x, first_z = 2 * zs, 3 * zs
    started = {}

    def put(src, dst, slot, peer):
        started[slot] = send(src, dst, send_sems, recv_sems, slot, peer)
        started[slot].start()

    for near in (0, 1):
        for k in order:
            slot = 2 * k + near
            block = at(k, near == 0, True)
            put(parts_ref.at[block], core_in.at[slot], slot, core_peer)

    def pair_sum(k, near):
        started[2 * k + near].wait_recv()
        return parts_ref[at(k, near == 0, False)].astype(jnp.float32) + core_in[
            2 * k + near
        ].astype(jnp.float32)

    for k in order:
        x_out[k] = pair_sum(k, 0).astype(jnp.bfloat16)
        put(x_out.at[k], x_in.at[k], first_x + k, x_peer)
    for k in order:
        total = pair_sum(k, 1)
        started[first_x + k].wait_recv()
        total = total + x_in[k].astype(jnp.float32)
        if k:
            z_out[k - 1] = total.astype(jnp.bfloat16)
            put(z_out.at[k - 1], z_in.at[k - 1], first_z + k - 1, at(k, False, False))
        else:
            sum_ref[...] = total
    for k in range(1, zs):
        started[first_z + k - 1].wait_recv()
        sum_ref[...] += z_in[k - 1].astype(jnp.float32)
    for slot in range(4 * zs - 1):
        started[slot].wait_send()


def reduce_all(parts, collective_id):
    tp_count, rows, cols = parts.shape
    zs = tp_count // 4
    copies = 4 * zs - 1
    return pl.pallas_call(
        lambda *refs: reduce_kernel(*refs, tp_count=tp_count),
        out_shape=jax.ShapeDtypeStruct((rows, cols), jnp.float32),
        in_specs=[pl.BlockSpec(memory_space=pltpu.VMEM)],
        out_specs=pl.BlockSpec(memory_space=pltpu.VMEM),
        scratch_shapes=[
            pltpu.VMEM((2 * zs, rows, cols), jnp.bfloat16),
            pltpu.VMEM((zs, rows, cols), jnp.bfloat16),
            pltpu.VMEM((zs, rows, cols), jnp.bfloat16),
            pltpu.VMEM((zs - 1, rows, cols), jnp.bfloat16),
            pltpu.VMEM((zs - 1, rows, cols), jnp.bfloat16),
            pltpu.SemaphoreType.DMA((copies,)),
            pltpu.SemaphoreType.DMA((copies,)),
        ],
        compiler_params=pltpu.CompilerParams(
            collective_id=collective_id,
            has_side_effects=True,
            vmem_limit_bytes=32 * 1024 * 1024,
        ),
    )(parts)


def take_pages(pages, owner_flat, target, capacity):
    mine = owner_flat == target
    rank = jnp.cumsum(mine.astype(jnp.int32)) - 1
    wanted = mine[None, :] & (rank[None, :] == jnp.arange(capacity)[:, None])
    picked = jnp.sum(jnp.where(wanted, jnp.arange(mine.shape[0])[None, :], 0), axis=1)
    filled = jnp.any(wanted, axis=1)
    taken = [lax.dynamic_index_in_dim(pages, picked[k], 0, True) for k in range(capacity)]
    return jnp.where(filled[:, None, None], jnp.concatenate(taken, axis=0), 0)


def body(hidden_in, attn_gain, w_query, w_keyval, w_out, cache, starts, owners):
    query_cols = w_query.shape[2]
    keyval_cols = w_keyval.shape[2]
    if query_cols != 2 * HD or keyval_cols != HD:
        return general_body(
            hidden_in, attn_gain, w_query, w_keyval, w_out, cache, starts, owners
        )
    tp_count = lax.axis_size("tp")
    section_count = lax.axis_size("section")
    tp_rank = lax.axis_index("tp")
    section_rank = lax.axis_index("section")
    local_rows = hidden_in.shape[1]
    heads_here = query_cols // HD
    scale = math.log2(math.e) / math.sqrt(HD)
    residual = hidden_in[0].astype(jnp.float32)
    normed = rms_norm(residual, attn_gain[0]).astype(jnp.bfloat16)
    all_rows = gather_all(normed, 0).reshape(FRESH, D)
    block_start = starts[0]
    positions = block_start + jnp.arange(FRESH, dtype=jnp.int32)
    queries = jnp.dot(all_rows, w_query[0], preferred_element_type=jnp.float32)
    queries = queries.astype(jnp.bfloat16).astype(jnp.float32)
    q_rot = rotate(queries.reshape(FRESH, heads_here, HD), positions).astype(jnp.bfloat16)
    q_rot = jnp.transpose(q_rot, (1, 0, 2))
    keyval = jnp.dot(all_rows, w_keyval[0], preferred_element_type=jnp.float32)
    keyval = keyval.astype(jnp.bfloat16)
    turned = rotate(keyval.astype(jnp.float32)[:, None, :], positions)[:, 0]
    holds_key = tp_rank % 2 == 0
    part = jnp.where(holds_key, turned.astype(jnp.bfloat16), keyval)
    pair = [(i, i ^ 1) for i in range(tp_count)]
    other = lax.ppermute(part, "tp", pair)
    fresh_key = jnp.where(holds_key, part, other)
    fresh_val = jnp.where(holds_key, other, part)

    step = local_rows // CHUNKS
    by_chunk = q_rot.reshape(heads_here, tp_count, CHUNKS, step, HD)
    part_rows = tp_count * step
    slots = cache.shape[2]
    count = jnp.clip(block_start - tp_rank * slots, 0, slots).reshape(1)
    local_cache = cache[0]
    token = jnp.arange(FRESH, dtype=jnp.int32).reshape(tp_count, CHUNKS, step)
    gathered = [
        gather_all(by_chunk[:, :, c].reshape(heads_here * part_rows, HD), 1 + 4 * c)
        for c in range(CHUNKS)
    ]
    outs = []
    for c in range(CHUNKS):
        q_all = gathered[c].reshape(KVH, H // KVH * part_rows, HD)
        sums, lse = attend(q_all, local_cache, count)
        sums = sums.reshape(H, part_rows, HD)
        lse = lse.reshape(H, part_rows)
        lses = gather_all(lse, 2 + 4 * c)
        peak = jnp.max(lses, axis=0)
        whole = peak + jnp.log2(jnp.sum(jnp.exp2(lses - peak[None]), axis=0))
        scaled = sums * jnp.exp2(lse - whole)[:, :, None]
        scaled = scaled.astype(jnp.bfloat16).reshape(tp_count, heads_here * part_rows, HD)
        share = reduce_all(scaled, 3 + 4 * c).reshape(heads_here, part_rows, HD)
        whole_here = lax.dynamic_slice_in_dim(whole, tp_rank * heads_here, heads_here, 0)
        mine = by_chunk[:, :, c].reshape(heads_here, part_rows, HD)
        new_scores = jnp.einsum(
            "hrd,kd->hrk", mine, fresh_key, preferred_element_type=jnp.float32
        )
        row_block = token[:, c].reshape(part_rows) // DBLOCK
        fresh_ok = jnp.arange(FRESH, dtype=jnp.int32)[None, :] // DBLOCK <= row_block[:, None]
        new_scores = jnp.where(fresh_ok[None], new_scores * scale, NEG)
        new_top = jnp.max(new_scores, axis=-1, keepdims=True)
        new_weights = jnp.exp2(new_scores - new_top)
        new_total = jnp.sum(new_weights, axis=-1)
        new_sums = jnp.einsum(
            "hrk,kd->hrd",
            new_weights.astype(jnp.bfloat16),
            fresh_val,
            preferred_element_type=jnp.float32,
        )
        joint = jnp.maximum(new_top[..., 0], whole_here)
        old_part = jnp.exp2(whole_here - joint)
        new_part = jnp.exp2(new_top[..., 0] - joint)
        attended = (share * old_part[..., None] + new_sums * new_part[..., None]) / (
            old_part + new_total * new_part
        )[..., None]
        attended = jnp.transpose(attended.astype(jnp.bfloat16), (1, 0, 2))
        attended = attended.reshape(part_rows, query_cols)
        product = jnp.dot(attended, w_out[0], preferred_element_type=jnp.float32)
        product = product.astype(jnp.bfloat16).reshape(tp_count, step, D)
        outs.append(reduce_all(product, 4 + 4 * c))
    projected_rows = jnp.stack(outs, axis=0).reshape(local_rows, D)
    layer_out = (residual + projected_rows).astype(jnp.bfloat16)
    passed_on = passed_along(layer_out, "section", 1)

    pages = lax.all_gather(part, ("section", "tp"), axis=0, tiled=True)
    pages = pages.reshape(-1, PAGE, HD)
    owner_flat = owners.reshape(-1)
    capacity = 3 * max(owner_flat.shape[0] // (section_count * tp_count), 1)
    self_index = section_rank * tp_count + tp_rank
    return (passed_on[None], take_pages(pages, owner_flat, self_index, capacity))


def solution(mesh):
    in_specs = (
        P("section", "tp", None),
        P("section", None),
        P("section", None, "tp"),
        P("section", None, "tp"),
        P("section", "tp", None),
        P("section", None, "tp", None),
        P("section"),
        P(),
    )
    out_specs = (P("section", "tp", None), P(("section", "tp"), None, None))
    return jax.shard_map(body, mesh=mesh, in_specs=in_specs, out_specs=out_specs, check_vma=False)
```

```python
import math

import jax
import jax.numpy as jnp
from jax import lax
from jax.experimental import pallas as pl
from jax.experimental.pallas import tpu as pltpu
from jax.sharding import PartitionSpec as P

D = 4096
H = 32
KVH = 8
HD = 128
PAGE = 128
DBLOCK = 4
FRESH = 512


def passed_along(block, axis, distance):
    devices = range(lax.axis_size(axis))
    route = [((i - distance) % len(devices), i) for i in devices]
    return lax.ppermute(block, axis, route)


def rms_norm(values, gain_vec):
    return values * lax.rsqrt(jnp.mean(values * values, axis=-1, keepdims=True) + 1e-06) * gain_vec


def rotate(vectors, positions):
    half_dim = vectors.shape[-1] // 2
    freq_index = jnp.arange(half_dim).astype(jnp.float32)
    inv_freq = jnp.exp(freq_index * (-2.0 * math.log(1000000.0) / vectors.shape[-1]))
    angles = positions.astype(jnp.float32)[:, None] * inv_freq[None, :]
    cosine = jnp.cos(angles)[:, None, :]
    sine = jnp.sin(angles)[:, None, :]
    first_half = vectors[..., :half_dim]
    second_half = vectors[..., half_dim:]
    return jnp.concatenate(
        [first_half * cosine - second_half * sine, second_half * cosine + first_half * sine],
        axis=-1,
    )


def pick_pages(page_set, owner_flat, section_slot, target, capacity):
    per_section = page_set.shape[0]
    is_mine = (owner_flat == target).astype(jnp.int32)
    slot_rank = jnp.cumsum(is_mine) - 1
    mine_here = lax.dynamic_slice_in_dim(is_mine, section_slot * per_section, per_section)
    rank_here = lax.dynamic_slice_in_dim(slot_rank, section_slot * per_section, per_section)
    wanted = (mine_here[None, :] == 1) & (rank_here[None, :] == jnp.arange(capacity)[:, None])
    return jnp.einsum(
        "cp,pxd->cxd", wanted.astype(jnp.bfloat16), page_set, preferred_element_type=jnp.float32
    )


def general_body(hidden_in, attn_gain, w_query, w_keyval, w_out, cache, starts, owners):
    tp_count = lax.axis_size("tp")
    section_count = lax.axis_size("section")
    tp_rank = lax.axis_index("tp")
    section_rank = lax.axis_index("section")
    group_size = H // KVH
    local_rows = hidden_in.shape[1]
    query_cols = w_query.shape[2]
    inv_scale = 1.0 / math.sqrt(HD)
    residual = hidden_in[0].astype(jnp.float32)
    normed = rms_norm(residual, attn_gain[0]).astype(jnp.bfloat16)
    query_weight = w_query[0]
    keyval_weight = w_keyval[0]
    rows_piece = lax.all_gather(normed, "tp", axis=0, tiled=True)
    projected = jnp.concatenate(
        [
            jnp.dot(rows_piece, query_weight, preferred_element_type=jnp.float32),
            jnp.dot(rows_piece, keyval_weight, preferred_element_type=jnp.float32),
        ],
        axis=1,
    )
    query_part = projected[:, :query_cols].astype(jnp.bfloat16)
    keyval_part = projected[:, query_cols:].astype(jnp.bfloat16)
    queries, keyval = (
        lax.all_gather(query_part, "tp", axis=1, tiled=True),
        lax.all_gather(keyval_part, "tp", axis=1, tiled=True),
    )
    block_start = starts[0]
    positions = block_start + jnp.arange(FRESH, dtype=jnp.int32)
    q_rot = rotate(queries.reshape(FRESH, H, HD).astype(jnp.float32), positions).astype(
        jnp.bfloat16
    )
    q_rot = q_rot.reshape(FRESH, KVH, group_size, HD)
    split_kv = keyval.reshape(FRESH, KVH, 2, HD)
    k_new = rotate(split_kv[:, :, 0].astype(jnp.float32), positions).astype(jnp.bfloat16)
    v_new = split_kv[:, :, 1]
    slot_count = cache.shape[2]
    fresh_count = FRESH // tp_count
    slot_positions = tp_rank * slot_count + jnp.arange(slot_count, dtype=jnp.int32)
    cached_ok = slot_positions < block_start
    fresh_index = tp_rank * fresh_count + jnp.arange(fresh_count, dtype=jnp.int32)
    row_block = jnp.arange(FRESH, dtype=jnp.int32) // DBLOCK
    fresh_ok = fresh_index[None, :] // DBLOCK <= row_block[:, None]
    fresh_keys = lax.dynamic_slice_in_dim(k_new, tp_rank * fresh_count, fresh_count, 0)
    fresh_vals = lax.dynamic_slice_in_dim(v_new, tp_rank * fresh_count, fresh_count, 0)
    local_cache = cache[0]

    def one_group(group_index, carry):
        tops, totals, sums = carry
        query_group = lax.dynamic_index_in_dim(q_rot, group_index, 1, False)
        cached = lax.dynamic_index_in_dim(local_cache, group_index, 0, False)
        cached_keys = cached[:, :HD]
        cached_vals = cached[:, HD:]
        new_keys = lax.dynamic_index_in_dim(fresh_keys, group_index, 1, False)
        new_vals = lax.dynamic_index_in_dim(fresh_vals, group_index, 1, False)
        cached_scores = (
            jnp.einsum("rqd,kd->rqk", query_group, cached_keys, preferred_element_type=jnp.float32)
            * inv_scale
        )
        new_scores = (
            jnp.einsum("rqd,kd->rqk", query_group, new_keys, preferred_element_type=jnp.float32)
            * inv_scale
        )
        cached_scores = jnp.where(cached_ok[None, None, :], cached_scores, -jnp.inf)
        new_scores = jnp.where(fresh_ok[:, None, :], new_scores, -jnp.inf)
        row_top = jnp.maximum(jnp.max(cached_scores, axis=-1), jnp.max(new_scores, axis=-1))
        shift_by = jnp.where(row_top > -jnp.inf, row_top, 0.0)
        cached_weights = jnp.exp(cached_scores - shift_by[..., None])
        new_weights = jnp.exp(new_scores - shift_by[..., None])
        weight_sum = jnp.sum(cached_weights, axis=-1) + jnp.sum(new_weights, axis=-1)
        value_sum = jnp.einsum(
            "rqk,kd->rqd",
            cached_weights.astype(jnp.bfloat16),
            cached_vals,
            preferred_element_type=jnp.float32,
        )
        value_sum = value_sum + jnp.einsum(
            "rqk,kd->rqd",
            new_weights.astype(jnp.bfloat16),
            new_vals,
            preferred_element_type=jnp.float32,
        )
        tops = lax.dynamic_update_index_in_dim(tops, row_top, group_index, 1)
        totals = lax.dynamic_update_index_in_dim(totals, weight_sum, group_index, 1)
        sums = lax.dynamic_update_index_in_dim(sums, value_sum, group_index, 1)
        return (tops, totals, sums)

    initial = (
        jnp.full((FRESH, KVH, group_size), -jnp.inf, jnp.float32),
        jnp.zeros((FRESH, KVH, group_size), jnp.float32),
        jnp.zeros((FRESH, KVH, group_size, HD), jnp.float32),
    )
    tops, totals, sums = lax.fori_loop(0, KVH, one_group, initial)
    tops = tops.reshape(FRESH, H)
    totals = totals.reshape(FRESH, H)
    peak = lax.pmax(tops.astype(jnp.bfloat16), "tp").astype(tops.dtype)
    factor = jnp.where(tops > -jnp.inf, jnp.exp(tops - peak), 0.0)
    scaled = (sums.reshape(FRESH, H, HD) * factor[:, :, None]).reshape(FRESH, D)
    head_share = lax.psum_scatter(scaled, "tp", scatter_dimension=1, tiled=True)
    weight_total = lax.psum(totals * factor, "tp")
    share_cols = head_share.shape[1]
    heads_here = max(share_cols // HD, 1)
    first_head = tp_rank * share_cols // HD
    denominator = lax.dynamic_slice_in_dim(weight_total, first_head, heads_here, 1)
    attended = (
        head_share.reshape(FRESH, heads_here, share_cols // heads_here) / denominator[:, :, None]
    )
    attended = attended.reshape(FRESH, share_cols).astype(jnp.bfloat16)
    out_weight = w_out[0]
    full_sum = lax.psum(jnp.dot(attended, out_weight, preferred_element_type=jnp.float32), "tp")
    projected_rows = lax.dynamic_slice_in_dim(full_sum, tp_rank * local_rows, local_rows, 0)
    layer_out = (residual + projected_rows).astype(jnp.bfloat16)
    passed_on = passed_along(layer_out, "section", 1)
    stacked = jnp.stack([k_new, v_new], axis=2).reshape(FRESH // PAGE, PAGE, KVH, 2, HD)
    local_pages = jnp.transpose(stacked, (2, 3, 0, 1, 4)).reshape(-1, PAGE, HD)
    owner_flat = owners.reshape(-1)
    capacity = 3 * max(owner_flat.shape[0] // (section_count * tp_count), 1)
    self_index = section_rank * tp_count + tp_rank
    page_slots = pick_pages(local_pages, owner_flat, section_rank, self_index, capacity)
    prior_section = (section_rank + section_count - 1) % section_count
    earlier_pages = passed_along(local_pages, "section", 1)
    page_slots = page_slots + pick_pages(
        earlier_pages, owner_flat, prior_section, self_index, capacity
    )
    return (passed_on[None], page_slots.astype(jnp.bfloat16))


NEG = -1e30
CHUNKS = 1
ROW_TILE = 256
TILES = 4


def attend_kernel(count_ref, q_ref, kv_ref, sums_ref, lse_ref, *, tile, scale):
    slots = kv_ref.shape[1]
    rows = q_ref.shape[1]
    count = count_ref[0]

    def run(masked):
        keys = kv_ref[0, :, :HD]
        vals = kv_ref[0, :, HD:]
        vals_one = jnp.concatenate([vals, jnp.ones_like(vals)], axis=1)
        if masked:
            seen = lax.broadcasted_iota(jnp.int32, (1, slots), 1) < count

        def scores_of(at):
            return lax.dot_general(
                q_ref[0, at * tile : (at + 1) * tile, :],
                keys,
                (((1,), (1,)), ((), ())),
                preferred_element_type=jnp.float32,
            )

        scores = scores_of(0)
        for at in range(rows // tile):
            later = scores_of(at + 1) if at + 1 < rows // tile else None
            if masked:
                scores = jnp.where(seen, scores, NEG)
            top = jnp.max(scores, axis=1, keepdims=True)
            weights = jnp.exp2((scores - top) * scale)
            if masked:
                weights = jnp.where(seen, weights, 0.0)
            both = jnp.dot(
                weights.astype(jnp.bfloat16), vals_one, preferred_element_type=jnp.float32
            )
            total = both[:, HD:]
            safe = jnp.where(total > 0.0, total, 1.0)
            sums_ref[0, at * tile : (at + 1) * tile, :] = both[:, :HD] / safe
            lse = jnp.where(total > 0.0, top * scale + jnp.log2(safe), NEG)
            lse_ref[0, 0:1, at * tile : (at + 1) * tile] = jnp.transpose(lse)[0:1, :]
            scores = later

    @pl.when(count == slots)
    def _():
        run(False)

    @pl.when((count > 0) & (count < slots))
    def _():
        run(True)

    @pl.when(count == 0)
    def _():
        sums_ref[...] = jnp.zeros_like(sums_ref)
        lse_ref[...] = jnp.full_like(lse_ref, NEG)


def attend(q_all, local_cache, count):
    groups, rows, _ = q_all.shape
    slots = local_cache.shape[1]
    tile = min(ROW_TILE, rows)
    block = min(tile * TILES, rows)
    scale = math.log2(math.e) / math.sqrt(HD)
    return pl.pallas_call(
        lambda *refs: attend_kernel(*refs, tile=tile, scale=scale),
        grid_spec=pltpu.PrefetchScalarGridSpec(
            num_scalar_prefetch=1,
            grid=(groups, rows // block),
            in_specs=[
                pl.BlockSpec((1, block, HD), lambda g, r, n: (g, r, 0)),
                pl.BlockSpec((1, slots, 2 * HD), lambda g, r, n: (g, 0, 0)),
            ],
            out_specs=[
                pl.BlockSpec((1, block, HD), lambda g, r, n: (g, r, 0)),
                pl.BlockSpec((1, 1, block), lambda g, r, n: (g, 0, r)),
            ],
        ),
        out_shape=[
            jax.ShapeDtypeStruct((groups, rows, HD), jnp.float32),
            jax.ShapeDtypeStruct((groups, 1, rows), jnp.float32),
        ],
        compiler_params=pltpu.CompilerParams(vmem_limit_bytes=50 * 1024 * 1024),
        cost_estimate=pl.CostEstimate(
            flops=4 * groups * rows * slots * HD,
            bytes_accessed=groups * slots * HD * 4 + groups * rows * HD * 6,
            transcendentals=groups * rows * slots,
        ),
    )(count, q_all, local_cache)


def places(tp_count):
    me = lax.axis_index("tp")
    zs = tp_count // 4
    core, x, z = me % 2, (me // 2) % 2, me // 4

    def at(step, flip_x, flip_core):
        x_at = 1 - x if flip_x else x
        core_at = 1 - core if flip_core else core
        return ((z + step + zs) % zs) * 4 + x_at * 2 + core_at

    return zs, at


def greet(peers):
    barrier = pltpu.get_barrier_semaphore()
    for peer in peers:
        pl.semaphore_signal(
            barrier, inc=1, device_id={"tp": peer}, device_id_type=pl.DeviceIdType.MESH
        )
    pl.semaphore_wait(barrier, len(peers))


def send(src, dst, send_sems, recv_sems, slot, peer):
    return pltpu.make_async_remote_copy(
        src_ref=src,
        dst_ref=dst,
        send_sem=send_sems.at[slot],
        recv_sem=recv_sems.at[slot],
        device_id={"tp": peer},
        device_id_type=pl.DeviceIdType.MESH,
    )


def gather_kernel(own_ref, all_ref, send_sems, recv_sems, own_sem, *, tp_count):
    zs, at = places(tp_count)
    me = at(0, False, False)
    x_peer, core_peer = at(0, True, False), at(0, False, True)
    greet([x_peer, core_peer] + [at(k, False, False) for k in range(1, zs)])
    first_x, first_core = zs - 1, 2 * zs - 1
    started = {}

    def put(src, block, slot, peer):
        started[slot] = send(src, all_ref.at[block], send_sems, recv_sems, slot, peer)
        started[slot].start()

    keep = pltpu.make_async_copy(own_ref, all_ref.at[me], own_sem)
    keep.start()
    put(own_ref, me, first_x, x_peer)
    for k in range(1, zs):
        put(own_ref, me, k - 1, at(k, False, False))
    put(own_ref, me, first_core, core_peer)
    order = [1, zs - 1] + list(range(2, zs - 1))

    def x_arrived(k):
        block = at(-k, True, False)
        started[first_x + k].wait_recv()
        put(all_ref.at[block], block, first_core + zs + k, core_peer)

    for k in order:
        block = at(-k, False, False)
        started[k - 1].wait_recv()
        put(all_ref.at[block], block, first_x + k, x_peer)
        put(all_ref.at[block], block, first_core + k, core_peer)
        if k == order[0]:
            x_arrived(0)
    for k in order:
        x_arrived(k)
    for slot in range(first_core, first_core + 2 * zs):
        started[slot].wait_recv()
    for slot in range(first_core + 2 * zs):
        started[slot].wait_send()
    keep.wait()


def gather_all(own, collective_id):
    tp_count = lax.axis_size("tp")
    copies = tp_count - 1
    return pl.pallas_call(
        lambda *refs: gather_kernel(*refs, tp_count=tp_count),
        out_shape=jax.ShapeDtypeStruct((tp_count,) + own.shape, own.dtype),
        in_specs=[pl.BlockSpec(memory_space=pl.ANY)],
        out_specs=pl.BlockSpec(memory_space=pl.ANY),
        scratch_shapes=[
            pltpu.SemaphoreType.DMA((copies,)),
            pltpu.SemaphoreType.DMA((copies,)),
            pltpu.SemaphoreType.DMA,
        ],
        compiler_params=pltpu.CompilerParams(
            collective_id=collective_id, has_side_effects=True
        ),
    )(own)


def reduce_kernel(
    parts_ref, sum_ref, core_in, x_out, x_in, z_out, z_in, send_sems, recv_sems, *, tp_count
):
    zs, at = places(tp_count)
    x_peer, core_peer = at(0, True, False), at(0, False, True)
    greet([x_peer, core_peer] + [at(k, False, False) for k in range(1, zs)])
    order = list(range(1, zs)) + [0]
    first_x, first_z = 2 * zs, 3 * zs
    started = {}

    def put(src, dst, slot, peer):
        started[slot] = send(src, dst, send_sems, recv_sems, slot, peer)
        started[slot].start()

    for near in (0, 1):
        for k in order:
            slot = 2 * k + near
            block = at(k, near == 0, True)
            put(parts_ref.at[block], core_in.at[slot], slot, core_peer)

    def pair_sum(k, near):
        started[2 * k + near].wait_recv()
        return parts_ref[at(k, near == 0, False)].astype(jnp.float32) + core_in[
            2 * k + near
        ].astype(jnp.float32)

    for k in order:
        x_out[k] = pair_sum(k, 0).astype(jnp.bfloat16)
        put(x_out.at[k], x_in.at[k], first_x + k, x_peer)
    for k in order:
        total = pair_sum(k, 1)
        started[first_x + k].wait_recv()
        total = total + x_in[k].astype(jnp.float32)
        if k:
            z_out[k - 1] = total.astype(jnp.bfloat16)
            put(z_out.at[k - 1], z_in.at[k - 1], first_z + k - 1, at(k, False, False))
        else:
            sum_ref[...] = total
    for k in range(1, zs):
        started[first_z + k - 1].wait_recv()
        sum_ref[...] += z_in[k - 1].astype(jnp.float32)
    for slot in range(4 * zs - 1):
        started[slot].wait_send()


def reduce_all(parts, collective_id):
    tp_count, rows, cols = parts.shape
    zs = tp_count // 4
    copies = 4 * zs - 1
    return pl.pallas_call(
        lambda *refs: reduce_kernel(*refs, tp_count=tp_count),
        out_shape=jax.ShapeDtypeStruct((rows, cols), jnp.float32),
        in_specs=[pl.BlockSpec(memory_space=pltpu.VMEM)],
        out_specs=pl.BlockSpec(memory_space=pltpu.VMEM),
        scratch_shapes=[
            pltpu.VMEM((2 * zs, rows, cols), jnp.bfloat16),
            pltpu.VMEM((zs, rows, cols), jnp.bfloat16),
            pltpu.VMEM((zs, rows, cols), jnp.bfloat16),
            pltpu.VMEM((zs - 1, rows, cols), jnp.bfloat16),
            pltpu.VMEM((zs - 1, rows, cols), jnp.bfloat16),
            pltpu.SemaphoreType.DMA((copies,)),
            pltpu.SemaphoreType.DMA((copies,)),
        ],
        compiler_params=pltpu.CompilerParams(
            collective_id=collective_id,
            has_side_effects=True,
            vmem_limit_bytes=32 * 1024 * 1024,
        ),
    )(parts)


def page_kernel(picks_ref, fills_ref, page_ref, slot_ref):
    keep = fills_ref[pl.program_id(0)] > 0

    @pl.when(keep)
    def _():
        slot_ref[...] = page_ref[...]

    @pl.when(jnp.logical_not(keep))
    def _():
        slot_ref[...] = jnp.zeros_like(slot_ref)


def take_pages(pages, owner_flat, target, capacity):
    mine = owner_flat == target
    rank = jnp.cumsum(mine.astype(jnp.int32)) - 1
    wanted = mine[None, :] & (rank[None, :] == jnp.arange(capacity)[:, None])
    picked = jnp.sum(jnp.where(wanted, jnp.arange(mine.shape[0])[None, :], 0), axis=1)
    filled = jnp.any(wanted, axis=1).astype(jnp.int32)
    return pl.pallas_call(
        page_kernel,
        grid_spec=pltpu.PrefetchScalarGridSpec(
            num_scalar_prefetch=2,
            grid=(capacity,),
            in_specs=[pl.BlockSpec((1, PAGE, HD), lambda k, picks, fills: (picks[k], 0, 0))],
            out_specs=pl.BlockSpec((1, PAGE, HD), lambda k, picks, fills: (k, 0, 0)),
        ),
        out_shape=jax.ShapeDtypeStruct((capacity, PAGE, HD), pages.dtype),
    )(picked, filled, pages)


def body(hidden_in, attn_gain, w_query, w_keyval, w_out, cache, starts, owners):
    query_cols = w_query.shape[2]
    keyval_cols = w_keyval.shape[2]
    if query_cols != 2 * HD or keyval_cols != HD:
        return general_body(
            hidden_in, attn_gain, w_query, w_keyval, w_out, cache, starts, owners
        )
    tp_count = lax.axis_size("tp")
    section_count = lax.axis_size("section")
    tp_rank = lax.axis_index("tp")
    section_rank = lax.axis_index("section")
    local_rows = hidden_in.shape[1]
    heads_here = query_cols // HD
    scale = math.log2(math.e) / math.sqrt(HD)
    residual = hidden_in[0].astype(jnp.float32)
    normed = rms_norm(residual, attn_gain[0]).astype(jnp.bfloat16)
    all_rows = gather_all(normed, 0).reshape(FRESH, D)
    block_start = starts[0]
    positions = block_start + jnp.arange(FRESH, dtype=jnp.int32)
    queries = jnp.dot(all_rows, w_query[0], preferred_element_type=jnp.float32)
    queries = queries.astype(jnp.bfloat16).astype(jnp.float32)
    q_rot = rotate(queries.reshape(FRESH, heads_here, HD), positions).astype(jnp.bfloat16)
    q_rot = jnp.transpose(q_rot, (1, 0, 2))
    keyval = jnp.dot(all_rows, w_keyval[0], preferred_element_type=jnp.float32)
    keyval = keyval.astype(jnp.bfloat16)
    turned = rotate(keyval.astype(jnp.float32)[:, None, :], positions)[:, 0]
    holds_key = tp_rank % 2 == 0
    part = jnp.where(holds_key, turned.astype(jnp.bfloat16), keyval)
    pair = [(i, i ^ 1) for i in range(tp_count)]
    other = lax.ppermute(part, "tp", pair)
    fresh_key = jnp.where(holds_key, part, other)
    fresh_val = jnp.where(holds_key, other, part)

    step = local_rows // CHUNKS
    by_chunk = q_rot.reshape(heads_here, tp_count, CHUNKS, step, HD)
    part_rows = tp_count * step
    slots = cache.shape[2]
    count = jnp.clip(block_start - tp_rank * slots, 0, slots).reshape(1)
    local_cache = cache[0]
    token = jnp.arange(FRESH, dtype=jnp.int32).reshape(tp_count, CHUNKS, step)
    gathered = [
        gather_all(by_chunk[:, :, c].reshape(heads_here * part_rows, HD), 1 + 4 * c)
        for c in range(CHUNKS)
    ]
    outs = []
    for c in range(CHUNKS):
        q_all = gathered[c].reshape(KVH, H // KVH * part_rows, HD)
        sums, lse = attend(q_all, local_cache, count)
        sums = sums.reshape(H, part_rows, HD)
        lse = lse.reshape(H, part_rows)
        lses = gather_all(lse, 2 + 4 * c)
        peak = jnp.max(lses, axis=0)
        whole = peak + jnp.log2(jnp.sum(jnp.exp2(lses - peak[None]), axis=0))
        scaled = sums * jnp.exp2(lse - whole)[:, :, None]
        scaled = scaled.astype(jnp.bfloat16).reshape(tp_count, heads_here * part_rows, HD)
        share = reduce_all(scaled, 3 + 4 * c).reshape(heads_here, part_rows, HD)
        whole_here = lax.dynamic_slice_in_dim(whole, tp_rank * heads_here, heads_here, 0)
        mine = by_chunk[:, :, c].reshape(heads_here, part_rows, HD)
        new_scores = jnp.einsum(
            "hrd,kd->hrk", mine, fresh_key, preferred_element_type=jnp.float32
        )
        row_block = token[:, c].reshape(part_rows) // DBLOCK
        fresh_ok = jnp.arange(FRESH, dtype=jnp.int32)[None, :] // DBLOCK <= row_block[:, None]
        new_scores = jnp.where(fresh_ok[None], new_scores * scale, NEG)
        new_top = jnp.max(new_scores, axis=-1, keepdims=True)
        new_weights = jnp.exp2(new_scores - new_top)
        new_total = jnp.sum(new_weights, axis=-1)
        new_sums = jnp.einsum(
            "hrk,kd->hrd",
            new_weights.astype(jnp.bfloat16),
            fresh_val,
            preferred_element_type=jnp.float32,
        )
        joint = jnp.maximum(new_top[..., 0], whole_here)
        old_part = jnp.exp2(whole_here - joint)
        new_part = jnp.exp2(new_top[..., 0] - joint)
        attended = (share * old_part[..., None] + new_sums * new_part[..., None]) / (
            old_part + new_total * new_part
        )[..., None]
        attended = jnp.transpose(attended.astype(jnp.bfloat16), (1, 0, 2))
        attended = attended.reshape(part_rows, query_cols)
        product = jnp.dot(attended, w_out[0], preferred_element_type=jnp.float32)
        product = product.astype(jnp.bfloat16).reshape(tp_count, step, D)
        outs.append(reduce_all(product, 4 + 4 * c))
    projected_rows = jnp.stack(outs, axis=0).reshape(local_rows, D)
    layer_out = (residual + projected_rows).astype(jnp.bfloat16)
    passed_on = passed_along(layer_out, "section", 1)

    part, _ = lax.optimization_barrier((part, gathered[0]))
    pages = lax.all_gather(part, ("section", "tp"), axis=0, tiled=True)
    pages = pages.reshape(-1, PAGE, HD)
    owner_flat = owners.reshape(-1)
    capacity = 3 * max(owner_flat.shape[0] // (section_count * tp_count), 1)
    self_index = section_rank * tp_count + tp_rank
    return (passed_on[None], take_pages(pages, owner_flat, self_index, capacity))


def solution(mesh):
    in_specs = (
        P("section", "tp", None),
        P("section", None),
        P("section", None, "tp"),
        P("section", None, "tp"),
        P("section", "tp", None),
        P("section", None, "tp", None),
        P("section"),
        P(),
    )
    out_specs = (P("section", "tp", None), P(("section", "tp"), None, None))
    return jax.shard_map(body, mesh=mesh, in_specs=in_specs, out_specs=out_specs, check_vma=False)
```
